32 devices in a mesh: pipe: 4 (over y, core), space: 8 (over z, x).
Axes of the slice: x: 2, y: 2, z: 4, core: 2. Of those that a mesh axis runs over, the one named last changes fastest.
Arguments:
- activations: bfloat16 [4, 64, 128, 2048], P('pipe', 'space'), may hold values from -6 to 6
- cotangent: bfloat16 [64, 128, 2048], P('space'), may hold values from -6 to 6
- w_first: bfloat16 [4, 2, 8, 256, 256], P('pipe'), may hold values from -0.25 to 0.25
- w_second: bfloat16 [4, 2, 8, 256, 256], P('pipe'), may hold values from -0.25 to 0.25
- b_first: float32 [4, 2, 2048], P('pipe'), may hold values from -1 to 1
Outputs:
- grads: bfloat16 [4, 64, 128, 2048], P('pipe', 'space')
The draws below stay inside these ranges and needn't reach their ends.
All inputs are finite; a program needn't handle non-finite values.
Results may differ from the reference program's by a relative error of at most 0.028.
Values may be sent and summed in bfloat16 or wider, within the bound.
A program may use at most 64 MiB of HBM per device.

```python
import jax
import jax.numpy as jnp
from jax import lax

H = 64
W = 128
NB = 8
BS = 256
C = 2048
SEGMENTS = 4


def shard_levels(stream_key, shape, cuts, smallest, high):
    def one(dim, blocks):
        steps = jax.random.uniform(jax.random.fold_in(jax.random.fold_in(stream_key, 6), dim), (blocks,), jnp.float32, smallest / len(cuts), high / len(cuts))
        return jnp.repeat(jnp.exp(steps), shape[dim] // blocks).reshape((-1,) + (1,) * (len(shape) - dim - 1))

    loudness = one(*cuts[0])
    for cut in cuts[1:]:
        loudness = loudness * one(*cut)
    return loudness


def bell_draw(own_key, dims, scale, most, shards=(), held_as=jnp.bfloat16):
    loudness = shard_levels(own_key, dims, shards, -0.22, 0.18) if shards else 1.0
    drawn = jax.random.normal(own_key, dims, jnp.float32) * scale * loudness
    return jnp.minimum(jnp.maximum(drawn, -most), most).astype(held_as)


def setup_inputs(seed: int = 0) -> dict:
    keys = jax.random.split(jax.random.key(seed), 6)
    return {
        "activations": bell_draw(keys[0], (SEGMENTS, H, W, C), 1.0, 6.0, ((0, 4), (1, 8))),
        "cotangent": bell_draw(keys[1], (H, W, C), 1.0, 6.0, ((0, 8),)),
        "w_first": bell_draw(keys[2], (SEGMENTS, 2, NB, BS, BS), (2 * BS) ** -0.5, 0.25, ((0, 4),)),
        "w_second": bell_draw(keys[3], (SEGMENTS, 2, NB, BS, BS), (2 * BS) ** -0.5, 0.25, ((0, 4),)),
        "b_first": jnp.clip(jax.random.uniform(keys[4], (SEGMENTS, 2, C), jnp.float32, -1.0, 1.0) * shard_levels(keys[4], (SEGMENTS, 2, C), ((0, 4),), -0.4, 0.0), -1.0, 1.0),
    }


def gelu_slope(values):
    return 0.5 * (1.0 + lax.erf(values * 0.7071067811865476)) + values * jnp.exp(-0.5 * values * values) * 0.3989422804014327


def spectrum(field_values, doubled):
    mode_count = W // 2
    along_rows = jnp.fft.rfft(field_values, axis=1, norm="ortho")[:, :mode_count]
    if doubled:
        factor = jnp.where(jnp.arange(mode_count) == 0, 1.0, 2.0).astype(jnp.float32)
        joined = along_rows * factor[None, :, None]
    else:
        part_real, part_imag = lax.optimization_barrier((jnp.real(along_rows).astype(jnp.bfloat16), jnp.imag(along_rows).astype(jnp.bfloat16)))
        joined = lax.complex(part_real.astype(jnp.float32), part_imag.astype(jnp.float32))
    full_modes = jnp.fft.fft(joined, axis=0, norm="ortho")
    return jnp.real(full_modes).astype(jnp.bfloat16), jnp.imag(full_modes).astype(jnp.bfloat16)


def inverse(grad_real, grad_imag):
    joined = lax.complex(grad_real.astype(jnp.float32), grad_imag.astype(jnp.float32))
    along_height = jnp.fft.ifft(joined, axis=0, norm="ortho")
    part_real, part_imag = lax.optimization_barrier((jnp.real(along_height).astype(jnp.bfloat16), jnp.imag(along_height).astype(jnp.bfloat16)))
    rejoined = lax.complex(part_real.astype(jnp.float32), part_imag.astype(jnp.float32))
    padded = jnp.pad(rejoined, ((0, 0), (0, W - W // 2), (0, 0)))
    return jnp.real(jnp.fft.ifft(padded, axis=1, norm="ortho"))


def blocked(operand, weights, transposed):
    pattern = "tnk,njk->tnj" if transposed else "tnj,njk->tnk"
    return jnp.einsum(pattern, operand.astype(jnp.float32), weights.astype(jnp.float32), precision=lax.Precision.HIGHEST)


def segment_back(activation, gradient, layer_one, layer_two, bias_one):
    token_count = H * (W // 2)
    spec_real, spec_imag = spectrum(activation.astype(jnp.float32), False)
    grad_real, grad_imag = spectrum(gradient, True)

    def to_tokens(values):
        return values.reshape(token_count, NB, BS)

    spec_real, spec_imag = to_tokens(spec_real), to_tokens(spec_imag)
    grad_real, grad_imag = to_tokens(grad_real), to_tokens(grad_imag)
    z_real = blocked(spec_real, layer_one[0], False) - blocked(spec_imag, layer_one[1], False) + bias_one[0].reshape(NB, BS)
    z_imag = blocked(spec_real, layer_one[1], False) + blocked(spec_imag, layer_one[0], False) + bias_one[1].reshape(NB, BS)
    adj_real = blocked(grad_real, layer_two[0], True) + blocked(grad_imag, layer_two[1], True)
    adj_imag = blocked(grad_imag, layer_two[0], True) - blocked(grad_real, layer_two[1], True)
    pre_real = (adj_real * gelu_slope(z_real)).astype(jnp.bfloat16)
    pre_imag = (adj_imag * gelu_slope(z_imag)).astype(jnp.bfloat16)
    src_real = (blocked(pre_real, layer_one[0], True) + blocked(pre_imag, layer_one[1], True)).astype(jnp.bfloat16)
    src_imag = (blocked(pre_imag, layer_one[0], True) - blocked(pre_real, layer_one[1], True)).astype(jnp.bfloat16)
    spatial = inverse(src_real.reshape(H, W // 2, NB * BS), src_imag.reshape(H, W // 2, NB * BS))
    return spatial + gradient


def reference(activations, cotangent, w_first, w_second, b_first):
    gradient = cotangent.astype(jnp.float32)
    collected = []
    for segment_index in range(SEGMENTS - 1, -1, -1):
        gradient = segment_back(activations[segment_index], gradient, w_first[segment_index], w_second[segment_index], b_first[segment_index])
        collected.append(gradient.astype(jnp.bfloat16))
    return jnp.stack(collected[::-1])
```

```python
import functools
import math

import jax
import jax.numpy as jnp
import numpy as np
from jax import lax
from jax.experimental import pallas as pl
from jax.experimental.pallas import tpu as pltpu
from jax.sharding import PartitionSpec as P

MESH = pl.DeviceIdType.MESH
BF16 = jnp.bfloat16
F32 = jnp.float32


def dft_tables(height, width, modes, ranks):
    rows = height // ranks
    cols = modes // ranks
    w = np.arange(width)
    k = np.arange(modes)
    wave = 2.0 * math.pi * ((k[:, None] * w[None, :]) % width) / width
    pair = np.stack([np.cos(wave), -np.sin(wave)], axis=1)
    row = np.einsum("kiw,hg->kihgw", pair, np.eye(rows))
    row = row.reshape(modes * 2 * rows, rows * width)
    h = np.arange(height)
    turn = 2.0 * math.pi * ((h[:, None] * h[None, :]) % height) / height
    c = np.cos(turn)
    s = np.sin(turn)
    full = np.stack([np.stack([c, s], axis=1), np.stack([-s, c], axis=1)])
    full = full.reshape(2, height, 2, ranks, rows)
    col = np.einsum("okish,mn->omksnih", full, np.eye(cols))
    col = col.reshape(2 * cols * height, ranks * cols * 2 * rows)
    flip = np.zeros((height, height))
    flip[h, (-h) % height] = 1.0
    return [jnp.asarray(t, BF16) for t in (row, col, col.T, row.T, flip)]


def gelu_slope(t):
    return (
        0.5 * (1.0 + lax.erf(t * 0.7071067811865476))
        + t * jnp.exp(-0.5 * t * t) * 0.3989422804014327
    )


def mm(a, b):
    return jnp.dot(a, b, preferred_element_type=F32)


def mmt(a, b):
    return lax.dot_general(a, b, (((1,), (1,)), ((), ())), preferred_element_type=F32)


def flat(x):
    ranks, rows, lanes = x.shape
    if rows % 16:
        return x.astype(F32).reshape(ranks * rows, lanes).astype(BF16)
    return x.reshape(ranks * rows, lanes)


def kernel(
    sizes,
    act_ref, cot_ref, first_ref, second_ref, bias_ref,
    row_ref, col_ref, icol_ref, irow_ref, flip_ref,
    out_ref,
    send_buf, recv_buf, back_buf, csend_buf, crecv_buf, g_buf, e_buf,
    a_ssem, a_rsem, b_ssem, b_rsem, c_ssem, c_rsem, g_ssem, g_rsem, e_ssem, e_rsem,
):
    ranks, stages, blocks, lanes, height, width = sizes
    me = lax.axis_index("space")
    stage = lax.axis_index("pipe")
    own = blocks // stages
    first_own = (stages - 1 - stage) * own
    tokens = g_buf.shape[1] // 2
    chunk = send_buf.shape[2]
    row_scale = 1.0 / math.sqrt(width)
    col_scale = 1.0 / math.sqrt(height)

    def columns(b):
        return pl.ds(pl.multiple_of(b * lanes, lanes), lanes)

    barrier = pltpu.get_barrier_semaphore()

    def greet_space(k, carry):
        pl.semaphore_signal(
            barrier, inc=1, device_id={"space": lax.rem(me + k, ranks)}, device_id_type=MESH
        )
        return carry

    def greet_pipe(k, carry):
        pl.semaphore_signal(
            barrier, inc=1, device_id={"pipe": lax.rem(stage + k, stages)}, device_id_type=MESH
        )
        return carry

    lax.fori_loop(1, ranks, greet_space, 0)
    lax.fori_loop(1, stages, greet_pipe, 0)
    pl.semaphore_wait(barrier, ranks + stages - 2)

    def scatter(value, sbuf, rbuf, ssem, rsem):
        sbuf[...] = value.reshape(ranks, chunk, lanes).astype(BF16)
        rbuf[me] = sbuf[me]

        def push(k, carry):
            peer = lax.rem(me + k, ranks)
            pltpu.make_async_remote_copy(
                src_ref=sbuf.at[peer],
                dst_ref=rbuf.at[me],
                send_sem=ssem,
                recv_sem=rsem,
                device_id={"space": peer},
                device_id_type=MESH,
            ).start()
            return carry

        lax.fori_loop(1, ranks, push, 0)

    def wait_all(buf, sem):
        part = buf.at[pl.ds(0, ranks - 1)]
        pltpu.make_async_copy(part, part, sem).wait()

    def wait_one(buf, sem):
        pltpu.make_async_copy(buf, buf, sem).wait()

    @pl.when(stage == stages - 1)
    def _():
        e_buf[...] = jnp.zeros_like(e_buf)

    def send_cot(j, carry):
        value = mm(row_ref[...], cot_ref[:, columns(first_own + j)]) * row_scale
        scatter(value, csend_buf.at[j], crecv_buf.at[j], c_ssem.at[j], c_rsem.at[j])
        return carry

    lax.fori_loop(0, own, send_cot, 0)

    def send_act(b, carry):
        value = mm(row_ref[...], act_ref[:, columns(b)]) * row_scale
        scatter(value, send_buf.at[b], recv_buf.at[b], a_ssem.at[b], a_rsem.at[b])
        return carry

    lax.fori_loop(0, blocks, send_act, 0)

    def make_grad(j, carry):
        b = first_own + j
        wait_all(crecv_buf.at[j], c_rsem.at[j])
        value = mm(col_ref[...], flat(crecv_buf[j])) * col_scale
        token = lax.rem(lax.broadcasted_iota(jnp.int32, value.shape, 0), tokens)
        mean = jnp.logical_and(token < height, me == 0)
        g_buf[b] = jnp.where(mean, value, 2.0 * value).astype(BF16)

        def push(k, inner):
            pltpu.make_async_remote_copy(
                src_ref=g_buf.at[b],
                dst_ref=g_buf.at[b],
                send_sem=g_ssem.at[j, k],
                recv_sem=g_rsem.at[b],
                device_id={"pipe": lax.rem(stage + k, stages)},
                device_id_type=MESH,
            ).start()
            return inner

        lax.fori_loop(1, stages, push, 0)
        return carry

    lax.fori_loop(0, own, make_grad, 0)

    def chain(b, carry):
        wait_all(recv_buf.at[b], a_rsem.at[b])
        spectra = (mm(col_ref[...], flat(recv_buf[b])) * col_scale).astype(BF16)
        s_re, s_im = spectra[:tokens], spectra[tokens:]
        a_re, a_im = first_ref[0, b], first_ref[1, b]
        slope_re = gelu_slope(mm(s_re, a_re) - mm(s_im, a_im) + bias_ref[0, b])
        slope_im = gelu_slope(mm(s_re, a_im) + mm(s_im, a_re) + bias_ref[1, b])

        mine = jnp.logical_and(b >= first_own, b < first_own + own)

        @pl.when(jnp.logical_not(mine))
        def _():
            wait_one(g_buf.at[b], g_rsem.at[b])

        @pl.when(stage < stages - 1)
        def _():
            wait_one(e_buf.at[b], e_rsem.at[b])

        e_re = e_buf[b, :tokens]
        e_im = e_buf[b, tokens:]
        flip = flip_ref[...]
        top_re = e_re[:height].astype(F32)
        top_im = e_im[:height].astype(F32)
        even_re = 0.5 * (top_re + mm(flip, e_re[:height]))
        even_im = 0.5 * (top_im - mm(flip, e_im[:height]))
        top_re = jnp.where(me == 0, even_re, top_re)
        top_im = jnp.where(me == 0, even_im, top_im)
        if tokens > height:
            add_re = jnp.concatenate([top_re, e_re[height:].astype(F32)], axis=0)
            add_im = jnp.concatenate([top_im, e_im[height:].astype(F32)], axis=0)
        else:
            add_re, add_im = top_re, top_im
        g_re = (g_buf[b, :tokens].astype(F32) + add_re).astype(BF16)
        g_im = (g_buf[b, tokens:].astype(F32) + add_im).astype(BF16)
        b_re, b_im = second_ref[0, b], second_ref[1, b]
        q_re = ((mmt(g_re, b_re) + mmt(g_im, b_im)) * slope_re).astype(BF16)
        q_im = ((mmt(g_im, b_re) - mmt(g_re, b_im)) * slope_im).astype(BF16)
        new_re = mmt(q_re, a_re) + mmt(q_im, a_im) + e_re.astype(F32)
        new_im = mmt(q_im, a_re) - mmt(q_re, a_im) + e_im.astype(F32)
        e_buf[b, :tokens] = new_re.astype(BF16)
        e_buf[b, tokens:] = new_im.astype(BF16)

        @pl.when(stage > 0)
        def _():
            pltpu.make_async_remote_copy(
                src_ref=e_buf.at[b],
                dst_ref=e_buf.at[b],
                send_sem=e_ssem.at[b],
                recv_sem=e_rsem.at[b],
                device_id={"pipe": lax.rem(stage + stages - 1, stages)},
                device_id_type=MESH,
            ).start()

        value = mm(icol_ref[...], e_buf[b]) * col_scale
        wait_all(send_buf.at[b], a_ssem.at[b])
        scatter(value, send_buf.at[b], back_buf.at[b], b_ssem.at[b], b_rsem.at[b])
        return carry

    lax.fori_loop(0, blocks, chain, 0)

    def finish(b, carry):
        wait_all(back_buf.at[b], b_rsem.at[b])
        value = mm(irow_ref[...], flat(back_buf[b])) * row_scale
        out_ref[:, columns(b)] = (cot_ref[:, columns(b)].astype(F32) + value).astype(BF16)
        wait_all(send_buf.at[b], b_ssem.at[b])

        @pl.when(stage > 0)
        def _():
            wait_one(e_buf.at[b], e_ssem.at[b])

        return carry

    lax.fori_loop(0, blocks, finish, 0)

    def drain(j, carry):
        wait_all(csend_buf.at[j], c_ssem.at[j])

        def one(k, inner):
            wait_one(g_buf.at[first_own + j], g_ssem.at[j, k])
            return inner

        lax.fori_loop(1, stages, one, 0)
        return carry

    lax.fori_loop(0, own, drain, 0)


def body(tables, activations, cotangent, w_first, w_second, b_first):
    ranks = lax.axis_size("space")
    stages = lax.axis_size("pipe")
    _, rows, width, channels = activations.shape
    blocks, lanes = w_first.shape[2], w_first.shape[3]
    height = rows * ranks
    cols = width // 2 // ranks
    own = blocks // stages
    chunk = 2 * cols * rows
    tokens = height * cols
    sizes = (ranks, stages, blocks, lanes, height, width)
    vmem = pl.BlockSpec(memory_space=pltpu.VMEM)
    wire = (blocks, ranks, chunk, lanes)
    dma = pltpu.SemaphoreType.DMA
    out = pl.pallas_call(
        functools.partial(kernel, sizes),
        out_shape=jax.ShapeDtypeStruct((rows * width, channels), BF16),
        in_specs=[vmem] * 10,
        out_specs=vmem,
        scratch_shapes=[
            pltpu.VMEM(wire, BF16),
            pltpu.VMEM(wire, BF16),
            pltpu.VMEM(wire, BF16),
            pltpu.VMEM((own,) + wire[1:], BF16),
            pltpu.VMEM((own,) + wire[1:], BF16),
            pltpu.VMEM((blocks, 2 * tokens, lanes), BF16),
            pltpu.VMEM((blocks, 2 * tokens, lanes), BF16),
            dma((blocks,)),
            dma((blocks,)),
            dma((blocks,)),
            dma((blocks,)),
            dma((own,)),
            dma((own,)),
            dma((own, stages)),
            dma((blocks,)),
            dma((blocks,)),
            dma((blocks,)),
        ],
        compiler_params=pltpu.CompilerParams(
            collective_id=0, has_side_effects=True, vmem_limit_bytes=62 * 1024 * 1024
        ),
    )(
        activations.reshape(rows * width, channels),
        cotangent.reshape(rows * width, channels),
        w_first[0],
        w_second[0],
        b_first[0].reshape(2, blocks, 1, lanes),
        *tables,
    )
    return out.reshape(activations.shape)


def solution(mesh):
    ranks = mesh.shape["space"]

    def run(activations, cotangent, w_first, w_second, b_first):
        height, width = activations.shape[1], activations.shape[2]
        tables = dft_tables(height, width, width // 2, ranks)
        inner = jax.shard_map(
            body,
            mesh=mesh,
            in_specs=(
                [P()] * 5,
                P("pipe", "space", None, None),
                P("space", None, None),
                P("pipe", None, None, None, None),
                P("pipe", None, None, None, None),
                P("pipe", None, None),
            ),
            out_specs=P("pipe", "space", None, None),
            check_vma=False,
        )
        return inner(tables, activations, cotangent, w_first, w_second, b_first)

    return run
```

```python
import functools
import math

import jax
import jax.numpy as jnp
import numpy as np
from jax import lax
from jax.experimental import pallas as pl
from jax.experimental.pallas import tpu as pltpu
from jax.sharding import PartitionSpec as P

MESH = pl.DeviceIdType.MESH
BF16 = jnp.bfloat16
F32 = jnp.float32


def dft_tables(height, width, modes, ranks):
    rows = height // ranks
    cols = modes // ranks
    w = np.arange(width)
    k = np.arange(modes)
    wave = 2.0 * math.pi * ((k[:, None] * w[None, :]) % width) / width
    pair = np.stack([np.cos(wave), -np.sin(wave)], axis=1)
    row = np.einsum("kiw,hg->kihgw", pair, np.eye(rows))
    row = row.reshape(modes * 2 * rows, rows * width)
    h = np.arange(height)
    turn = 2.0 * math.pi * ((h[:, None] * h[None, :]) % height) / height
    c = np.cos(turn)
    s = np.sin(turn)
    full = np.stack([np.stack([c, s], axis=1), np.stack([-s, c], axis=1)])
    full = full.reshape(2, height, 2, ranks, rows)
    col = np.einsum("okish,mn->omksnih", full, np.eye(cols))
    col = col.reshape(2 * cols * height, ranks * cols * 2 * rows)
    flip = np.zeros((height, height))
    flip[h, (-h) % height] = 1.0
    return [jnp.asarray(t, BF16) for t in (row, col, col.T, row.T, flip)]


def gelu_slope(t):
    return (
        0.5 * (1.0 + lax.erf(t * 0.7071067811865476))
        + t * jnp.exp(-0.5 * t * t) * 0.3989422804014327
    )


def mm(a, b):
    return jnp.dot(a, b, preferred_element_type=F32)


def mmt(a, b):
    return lax.dot_general(a, b, (((1,), (1,)), ((), ())), preferred_element_type=F32)


def flat(x):
    ranks, rows, lanes = x.shape
    if rows % 16:
        return x.astype(F32).reshape(ranks * rows, lanes).astype(BF16)
    return x.reshape(ranks * rows, lanes)


def kernel(
    sizes,
    act_hbm, cot_hbm, first_hbm, second_hbm, bias_ref,
    row_hbm, col_hbm, icol_hbm, irow_hbm, flip_ref,
    out_hbm,
    act_ref, cot_ref, first_ref, second_ref, row_ref, col_ref, icol_ref, irow_ref,
    act_sem, cot_sem, load_sem, out_sem,
    send_buf, recv_buf, back_buf, csend_buf, crecv_buf, g_buf, e_buf,
    a_ssem, a_rsem, b_ssem, b_rsem, c_ssem, c_rsem, g_ssem, g_rsem, e_ssem, e_rsem,
):
    ranks, stages, blocks, lanes, height, width = sizes
    me = lax.axis_index("space")
    stage = lax.axis_index("pipe")
    own = blocks // stages
    first_own = (stages - 1 - stage) * own
    tokens = g_buf.shape[1] // 2
    chunk = send_buf.shape[2]
    row_scale = 1.0 / math.sqrt(width)
    col_scale = 1.0 / math.sqrt(height)

    def columns(b):
        return pl.ds(pl.multiple_of(b * lanes, lanes), lanes)

    loads = [
        pltpu.make_async_copy(src, dst, load_sem.at[i])
        for i, (src, dst) in enumerate(
            [
                (row_hbm, row_ref),
                (col_hbm, col_ref),
                (first_hbm, first_ref),
                (second_hbm, second_ref),
                (icol_hbm, icol_ref),
                (irow_hbm, irow_ref),
            ]
        )
    ]

    def load_act(b):
        part = columns(b)
        return pltpu.make_async_copy(act_hbm.at[:, part], act_ref.at[:, part], act_sem.at[b])

    def load_cot(b):
        part = columns(b)
        return pltpu.make_async_copy(cot_hbm.at[:, part], cot_ref.at[:, part], cot_sem.at[b])

    def store_out(b):
        part = columns(b)
        return pltpu.make_async_copy(act_ref.at[:, part], out_hbm.at[:, part], out_sem.at[b])

    def each(low, high, act):
        def step(i, carry):
            act(i)
            return carry

        lax.fori_loop(low, high, step, 0)

    loads[0].start()
    each(0, own, lambda j: load_cot(first_own + j).start())
    each(0, blocks, lambda b: load_act(b).start())
    for load in loads[1:]:
        load.start()
    each(own, blocks, lambda j: load_cot(lax.rem(first_own + j, blocks)).start())

    barrier = pltpu.get_barrier_semaphore()

    def greet_space(k, carry):
        pl.semaphore_signal(
            barrier, inc=1, device_id={"space": lax.rem(me + k, ranks)}, device_id_type=MESH
        )
        return carry

    def greet_pipe(k, carry):
        pl.semaphore_signal(
            barrier, inc=1, device_id={"pipe": lax.rem(stage + k, stages)}, device_id_type=MESH
        )
        return carry

    lax.fori_loop(1, ranks, greet_space, 0)
    lax.fori_loop(1, stages, greet_pipe, 0)
    pl.semaphore_wait(barrier, ranks + stages - 2)

    def scatter(value, sbuf, rbuf, ssem, rsem):
        sbuf[...] = value.reshape(ranks, chunk, lanes).astype(BF16)
        rbuf[me] = sbuf[me]

        def push(k, carry):
            peer = lax.rem(me + k, ranks)
            pltpu.make_async_remote_copy(
                src_ref=sbuf.at[peer],
                dst_ref=rbuf.at[me],
                send_sem=ssem,
                recv_sem=rsem,
                device_id={"space": peer},
                device_id_type=MESH,
            ).start()
            return carry

        lax.fori_loop(1, ranks, push, 0)

    def wait_all(buf, sem):
        part = buf.at[pl.ds(0, ranks - 1)]
        pltpu.make_async_copy(part, part, sem).wait()

    def wait_one(buf, sem):
        pltpu.make_async_copy(buf, buf, sem).wait()

    @pl.when(stage == stages - 1)
    def _():
        e_buf[...] = jnp.zeros_like(e_buf)

    loads[0].wait()

    def send_cot(j, carry):
        load_cot(first_own + j).wait()
        value = mm(row_ref[...], cot_ref[:, columns(first_own + j)]) * row_scale
        scatter(value, csend_buf.at[j], crecv_buf.at[j], c_ssem.at[j], c_rsem.at[j])
        return carry

    lax.fori_loop(0, own, send_cot, 0)

    def send_act(b, carry):
        load_act(b).wait()
        value = mm(row_ref[...], act_ref[:, columns(b)]) * row_scale
        scatter(value, send_buf.at[b], recv_buf.at[b], a_ssem.at[b], a_rsem.at[b])
        return carry

    lax.fori_loop(0, blocks, send_act, 0)

    loads[1].wait()

    def make_grad(j, carry):
        b = first_own + j
        wait_all(crecv_buf.at[j], c_rsem.at[j])
        value = mm(col_ref[...], flat(crecv_buf[j])) * col_scale
        token = lax.rem(lax.broadcasted_iota(jnp.int32, value.shape, 0), tokens)
        mean = jnp.logical_and(token < height, me == 0)
        g_buf[b] = jnp.where(mean, value, 2.0 * value).astype(BF16)

        def push(k, inner):
            pltpu.make_async_remote_copy(
                src_ref=g_buf.at[b],
                dst_ref=g_buf.at[b],
                send_sem=g_ssem.at[j, k],
                recv_sem=g_rsem.at[b],
                device_id={"pipe": lax.rem(stage + k, stages)},
                device_id_type=MESH,
            ).start()
            return inner

        lax.fori_loop(1, stages, push, 0)
        return carry

    lax.fori_loop(0, own, make_grad, 0)

    for load in loads[2:5]:
        load.wait()

    def chain(b, carry):
        wait_all(recv_buf.at[b], a_rsem.at[b])
        spectra = (mm(col_ref[...], flat(recv_buf[b])) * col_scale).astype(BF16)
        s_re, s_im = spectra[:tokens], spectra[tokens:]
        a_re, a_im = first_ref[0, b], first_ref[1, b]
        slope_re = gelu_slope(mm(s_re, a_re) - mm(s_im, a_im) + bias_ref[0, 0:1, columns(b)])
        slope_im = gelu_slope(mm(s_re, a_im) + mm(s_im, a_re) + bias_ref[0, 1:2, columns(b)])

        mine = jnp.logical_and(b >= first_own, b < first_own + own)

        @pl.when(jnp.logical_not(mine))
        def _():
            wait_one(g_buf.at[b], g_rsem.at[b])

        @pl.when(stage < stages - 1)
        def _():
            wait_one(e_buf.at[b], e_rsem.at[b])

        e_re = e_buf[b, :tokens]
        e_im = e_buf[b, tokens:]
        flip = flip_ref[...]
        top_re = e_re[:height].astype(F32)
        top_im = e_im[:height].astype(F32)
        even_re = 0.5 * (top_re + mm(flip, e_re[:height]))
        even_im = 0.5 * (top_im - mm(flip, e_im[:height]))
        top_re = jnp.where(me == 0, even_re, top_re)
        top_im = jnp.where(me == 0, even_im, top_im)
        if tokens > height:
            add_re = jnp.concatenate([top_re, e_re[height:].astype(F32)], axis=0)
            add_im = jnp.concatenate([top_im, e_im[height:].astype(F32)], axis=0)
        else:
            add_re, add_im = top_re, top_im
        g_re = (g_buf[b, :tokens].astype(F32) + add_re).astype(BF16)
        g_im = (g_buf[b, tokens:].astype(F32) + add_im).astype(BF16)
        b_re, b_im = second_ref[0, b], second_ref[1, b]
        q_re = ((mmt(g_re, b_re) + mmt(g_im, b_im)) * slope_re).astype(BF16)
        q_im = ((mmt(g_im, b_re) - mmt(g_re, b_im)) * slope_im).astype(BF16)
        new_re = mmt(q_re, a_re) + mmt(q_im, a_im) + e_re.astype(F32)
        new_im = mmt(q_im, a_re) - mmt(q_re, a_im) + e_im.astype(F32)
        e_buf[b, :tokens] = new_re.astype(BF16)
        e_buf[b, tokens:] = new_im.astype(BF16)

        @pl.when(stage > 0)
        def _():
            pltpu.make_async_remote_copy(
                src_ref=e_buf.at[b],
                dst_ref=e_buf.at[b],
                send_sem=e_ssem.at[b],
                recv_sem=e_rsem.at[b],
                device_id={"pipe": lax.rem(stage + stages - 1, stages)},
                device_id_type=MESH,
            ).start()

        value = mm(icol_ref[...], e_buf[b]) * col_scale
        wait_all(send_buf.at[b], a_ssem.at[b])
        scatter(value, send_buf.at[b], back_buf.at[b], b_ssem.at[b], b_rsem.at[b])
        return carry

    lax.fori_loop(0, blocks, chain, 0)

    loads[5].wait()
    each(own, blocks, lambda j: load_cot(lax.rem(first_own + j, blocks)).wait())

    def finish(b, carry):
        wait_all(back_buf.at[b], b_rsem.at[b])
        value = mm(irow_ref[...], flat(back_buf[b])) * row_scale
        act_ref[:, columns(b)] = (cot_ref[:, columns(b)].astype(F32) + value).astype(BF16)
        store_out(b).start()
        wait_all(send_buf.at[b], b_ssem.at[b])

        @pl.when(stage > 0)
        def _():
            wait_one(e_buf.at[b], e_ssem.at[b])

        return carry

    lax.fori_loop(0, blocks, finish, 0)

    def drain(j, carry):
        wait_all(csend_buf.at[j], c_ssem.at[j])

        def one(k, inner):
            wait_one(g_buf.at[first_own + j], g_ssem.at[j, k])
            return inner

        lax.fori_loop(1, stages, one, 0)
        return carry

    lax.fori_loop(0, own, drain, 0)
    each(0, blocks, lambda b: store_out(b).wait())


def body(tables, activations, cotangent, w_first, w_second, b_first):
    ranks = lax.axis_size("space")
    stages = lax.axis_size("pipe")
    _, rows, width, channels = activations.shape
    blocks, lanes = w_first.shape[2], w_first.shape[3]
    height = rows * ranks
    cols = width // 2 // ranks
    own = blocks // stages
    chunk = 2 * cols * rows
    tokens = height * cols
    sizes = (ranks, stages, blocks, lanes, height, width)
    vmem = pl.BlockSpec(memory_space=pltpu.VMEM)
    hbm = pl.BlockSpec(memory_space=pl.ANY)
    wire = (blocks, ranks, chunk, lanes)
    dma = pltpu.SemaphoreType.DMA
    out = pl.pallas_call(
        functools.partial(kernel, sizes),
        out_shape=jax.ShapeDtypeStruct((rows * width, channels), BF16),
        in_specs=[hbm] * 4 + [vmem] + [hbm] * 4 + [vmem],
        out_specs=hbm,
        scratch_shapes=[
            pltpu.VMEM((rows * width, channels), BF16),
            pltpu.VMEM((rows * width, channels), BF16),
            pltpu.VMEM(w_first.shape[1:], BF16),
            pltpu.VMEM(w_second.shape[1:], BF16),
            *[pltpu.VMEM(t.shape, BF16) for t in tables[:4]],
            dma((blocks,)),
            dma((blocks,)),
            dma((6,)),
            dma((blocks,)),
            pltpu.VMEM(wire, BF16),
            pltpu.VMEM(wire, BF16),
            pltpu.VMEM(wire, BF16),
            pltpu.VMEM((own,) + wire[1:], BF16),
            pltpu.VMEM((own,) + wire[1:], BF16),
            pltpu.VMEM((blocks, 2 * tokens, lanes), BF16),
            pltpu.VMEM((blocks, 2 * tokens, lanes), BF16),
            dma((blocks,)),
            dma((blocks,)),
            dma((blocks,)),
            dma((blocks,)),
            dma((own,)),
            dma((own,)),
            dma((own, stages)),
            dma((blocks,)),
            dma((blocks,)),
            dma((blocks,)),
        ],
        compiler_params=pltpu.CompilerParams(
            collective_id=0, has_side_effects=True, vmem_limit_bytes=62 * 1024 * 1024
        ),
    )(
        activations.reshape(rows * width, channels),
        cotangent.reshape(rows * width, channels),
        w_first[0],
        w_second[0],
        b_first,
        *tables,
    )
    return out.reshape(activations.shape)


def solution(mesh):
    ranks = mesh.shape["space"]

    def run(activations, cotangent, w_first, w_second, b_first):
        height, width = activations.shape[1], activations.shape[2]
        tables = dft_tables(height, width, width // 2, ranks)
        inner = jax.shard_map(
            body,
            mesh=mesh,
            in_specs=(
                [P()] * 5,
                P("pipe", "space", None, None),
                P("space", None, None),
                P("pipe", None, None, None, None),
                P("pipe", None, None, None, None),
                P("pipe", None, None),
            ),
            out_specs=P("pipe", "space", None, None),
            check_vma=False,
        )
        return inner(tables, activations, cotangent, w_first, w_second, b_first)

    return run
```

```python
import functools
import math

import jax
import jax.numpy as jnp
import numpy as np
from jax import lax
from jax.experimental import pallas as pl
from jax.experimental.pallas import tpu as pltpu
from jax.sharding import PartitionSpec as P

MESH = pl.DeviceIdType.MESH
BF16 = jnp.bfloat16
F32 = jnp.float32


def dft_tables(height, width, modes, ranks):
    rows = height // ranks
    cols = modes // ranks
    w = np.arange(width)
    k = np.arange(modes)
    wave = 2.0 * math.pi * ((k[:, None] * w[None, :]) % width) / width
    pair = np.stack([np.cos(wave), -np.sin(wave)], axis=1)
    row = np.einsum("kiw,hg->kihgw", pair, np.eye(rows))
    row = row.reshape(modes * 2 * rows, rows * width)
    h = np.arange(height)
    turn = 2.0 * math.pi * ((h[:, None] * h[None, :]) % height) / height
    c = np.cos(turn)
    s = np.sin(turn)
    full = np.stack([np.stack([c, s], axis=1), np.stack([-s, c], axis=1)])
    full = full.reshape(2, height, 2, ranks, rows)
    col = np.einsum("okish,mn->omksnih", full, np.eye(cols))
    col = col.reshape(2 * cols * height, ranks * cols * 2 * rows)
    flip = np.zeros((height, height))
    flip[h, (-h) % height] = 1.0
    return [jnp.asarray(t, BF16) for t in (row, col, col.T, row.T, flip)]


def gelu_slope(t):
    return (
        0.5 * (1.0 + lax.erf(t * 0.7071067811865476))
        + t * jnp.exp(-0.5 * t * t) * 0.3989422804014327
    )


def mm(a, b):
    return jnp.dot(a, b, preferred_element_type=F32)


def mmt(a, b):
    return lax.dot_general(a, b, (((1,), (1,)), ((), ())), preferred_element_type=F32)


def flat(x):
    ranks, rows, lanes = x.shape
    if rows % 16:
        return x.astype(F32).reshape(ranks * rows, lanes).astype(BF16)
    return x.reshape(ranks * rows, lanes)


def kernel(
    sizes,
    act_hbm, cot_hbm, first_hbm, second_hbm, bias_ref,
    row_hbm, col_hbm, icol_hbm, irow_hbm, flip_ref,
    out_hbm,
    act_ref, cot_ref, first_ref, second_ref, row_ref, col_ref, icol_ref, irow_ref,
    act_sem, cot_sem, load_sem, out_sem,
    send_buf, recv_buf, back_buf, csend_buf, crecv_buf, g_buf, e_buf,
    a_ssem, a_rsem, b_ssem, b_rsem, c_ssem, c_rsem, g_ssem, g_rsem, e_ssem, e_rsem,
):
    ranks, stages, blocks, lanes, height, width = sizes
    me = lax.axis_index("space")
    stage = lax.axis_index("pipe")
    own = blocks // stages
    first_own = (stages - 1 - stage) * own
    tokens = g_buf.shape[1] // 2
    chunk = send_buf.shape[2]
    row_scale = 1.0 / math.sqrt(width)
    col_scale = 1.0 / math.sqrt(height)

    def columns(b):
        return pl.ds(pl.multiple_of(b * lanes, lanes), lanes)

    loads = [
        pltpu.make_async_copy(src, dst, load_sem.at[i])
        for i, (src, dst) in enumerate(
            [
                (row_hbm, row_ref),
                (col_hbm, col_ref),
                (first_hbm, first_ref),
                (second_hbm, second_ref),
                (icol_hbm, icol_ref),
                (irow_hbm, irow_ref),
            ]
        )
    ]

    def load_act(b):
        part = columns(b)
        return pltpu.make_async_copy(act_hbm.at[:, part], act_ref.at[:, part], act_sem.at[b])

    def load_cot(b):
        part = columns(b)
        return pltpu.make_async_copy(cot_hbm.at[:, part], cot_ref.at[:, part], cot_sem.at[b])

    def store_out(b):
        part = columns(b)
        return pltpu.make_async_copy(act_ref.at[:, part], out_hbm.at[:, part], out_sem.at[b])

    def each(low, high, act):
        def step(i, carry):
            act(i)
            return carry

        lax.fori_loop(low, high, step, 0)

    loads[0].start()
    each(0, own, lambda j: load_cot(first_own + j).start())
    each(0, blocks, lambda b: load_act(b).start())
    for load in loads[1:]:
        load.start()
    each(own, blocks, lambda j: load_cot(lax.rem(first_own + j, blocks)).start())

    barrier = pltpu.get_barrier_semaphore()

    def greet_space(k, carry):
        pl.semaphore_signal(
            barrier, inc=1, device_id={"space": lax.rem(me + k, ranks)}, device_id_type=MESH
        )
        return carry

    def greet_pipe(k, carry):
        pl.semaphore_signal(
            barrier, inc=1, device_id={"pipe": lax.rem(stage + k, stages)}, device_id_type=MESH
        )
        return carry

    lax.fori_loop(1, ranks, greet_space, 0)
    lax.fori_loop(1, stages, greet_pipe, 0)
    pl.semaphore_wait(barrier, ranks + stages - 2)

    def scatter(value, sbuf, rbuf, ssem, rsem):
        sbuf[...] = value.reshape(ranks, chunk, lanes).astype(BF16)
        rbuf[me] = sbuf[me]

        def push(k, carry):
            peer = lax.rem(me + k, ranks)
            pltpu.make_async_remote_copy(
                src_ref=sbuf.at[peer],
                dst_ref=rbuf.at[me],
                send_sem=ssem,
                recv_sem=rsem,
                device_id={"space": peer},
                device_id_type=MESH,
            ).start()
            return carry

        lax.fori_loop(1, ranks, push, 0)

    def wait_all(buf, sem):
        part = buf.at[pl.ds(0, ranks - 1)]
        pltpu.make_async_copy(part, part, sem).wait()

    def wait_one(buf, sem):
        pltpu.make_async_copy(buf, buf, sem).wait()

    @pl.when(stage == stages - 1)
    def _():
        e_buf[...] = jnp.zeros_like(e_buf)

    loads[0].wait()

    def send_cot(j, carry):
        load_cot(first_own + j).wait()
        value = mm(row_ref[...], cot_ref[:, columns(first_own + j)]) * row_scale
        scatter(value, csend_buf.at[j], crecv_buf.at[j], c_ssem.at[j], c_rsem.at[j])
        return carry

    lax.fori_loop(0, own, send_cot, 0)

    def send_act(b, carry):
        load_act(b).wait()
        value = mm(row_ref[...], act_ref[:, columns(b)]) * row_scale
        scatter(value, send_buf.at[b], recv_buf.at[b], a_ssem.at[b], a_rsem.at[b])
        return carry

    lax.fori_loop(0, blocks, send_act, 0)

    loads[1].wait()

    def make_grad(j, carry):
        b = first_own + j
        wait_all(crecv_buf.at[j], c_rsem.at[j])
        value = mm(col_ref[...], flat(crecv_buf[j])) * col_scale
        token = lax.rem(lax.broadcasted_iota(jnp.int32, value.shape, 0), tokens)
        mean = jnp.logical_and(token < height, me == 0)
        g_buf[b] = jnp.where(mean, value, 2.0 * value).astype(BF16)

        def push(k, inner):
            pltpu.make_async_remote_copy(
                src_ref=g_buf.at[b],
                dst_ref=g_buf.at[b],
                send_sem=g_ssem.at[j, k],
                recv_sem=g_rsem.at[b],
                device_id={"pipe": lax.rem(stage + k, stages)},
                device_id_type=MESH,
            ).start()
            return inner

        lax.fori_loop(1, stages, push, 0)
        return carry

    lax.fori_loop(0, own, make_grad, 0)

    for load in loads[2:5]:
        load.wait()

    def chain(b, carry):
        wait_all(recv_buf.at[b], a_rsem.at[b])
        spectra = (mm(col_ref[...], flat(recv_buf[b])) * col_scale).astype(BF16)
        s_re, s_im = spectra[:tokens], spectra[tokens:]
        a_re, a_im = first_ref[0, b], first_ref[1, b]
        slope_re = gelu_slope(mm(s_re, a_re) - mm(s_im, a_im) + bias_ref[0, 0:1, columns(b)])
        slope_im = gelu_slope(mm(s_re, a_im) + mm(s_im, a_re) + bias_ref[0, 1:2, columns(b)])

        mine = jnp.logical_and(b >= first_own, b < first_own + own)

        @pl.when(jnp.logical_not(mine))
        def _():
            wait_one(g_buf.at[b], g_rsem.at[b])

        @pl.when(stage < stages - 1)
        def _():
            wait_one(e_buf.at[b], e_rsem.at[b])

        e_re = e_buf[b, :tokens]
        e_im = e_buf[b, tokens:]
        flip = flip_ref[...]
        top_re = e_re[:height].astype(F32)
        top_im = e_im[:height].astype(F32)
        even_re = 0.5 * (top_re + mm(flip, e_re[:height]))
        even_im = 0.5 * (top_im - mm(flip, e_im[:height]))
        top_re = jnp.where(me == 0, even_re, top_re)
        top_im = jnp.where(me == 0, even_im, top_im)
        if tokens > height:
            add_re = jnp.concatenate([top_re, e_re[height:].astype(F32)], axis=0)
            add_im = jnp.concatenate([top_im, e_im[height:].astype(F32)], axis=0)
        else:
            add_re, add_im = top_re, top_im
        g_re = (g_buf[b, :tokens].astype(F32) + add_re).astype(BF16)
        g_im = (g_buf[b, tokens:].astype(F32) + add_im).astype(BF16)
        b_re, b_im = second_ref[0, b], second_ref[1, b]
        q_re = ((mmt(g_re, b_re) + mmt(g_im, b_im)) * slope_re).astype(BF16)
        q_im = ((mmt(g_im, b_re) - mmt(g_re, b_im)) * slope_im).astype(BF16)
        new_re = mmt(q_re, a_re) + mmt(q_im, a_im) + e_re.astype(F32)
        new_im = mmt(q_im, a_re) - mmt(q_re, a_im) + e_im.astype(F32)
        e_buf[b, :tokens] = new_re.astype(BF16)
        e_buf[b, tokens:] = new_im.astype(BF16)

        @pl.when(stage > 0)
        def _():
            pltpu.make_async_remote_copy(
                src_ref=e_buf.at[b],
                dst_ref=e_buf.at[b],
                send_sem=e_ssem.at[b],
                recv_sem=e_rsem.at[b],
                device_id={"pipe": lax.rem(stage + stages - 1, stages)},
                device_id_type=MESH,
            ).start()

        value = mm(icol_ref[...], e_buf[b]) * col_scale
        wait_all(send_buf.at[b], a_ssem.at[b])
        scatter(value, send_buf.at[b], back_buf.at[b], b_ssem.at[b], b_rsem.at[b])
        return carry

    lax.fori_loop(0, blocks, chain, 0)

    loads[5].wait()
    each(own, blocks, lambda j: load_cot(lax.rem(first_own + j, blocks)).wait())

    def finish(b, carry):
        wait_all(back_buf.at[b], b_rsem.at[b])
        value = mm(irow_ref[...], flat(back_buf[b])) * row_scale
        act_ref[:, columns(b)] = (cot_ref[:, columns(b)].astype(F32) + value).astype(BF16)
        store_out(b).start()
        wait_all(send_buf.at[b], b_ssem.at[b])

        @pl.when(stage > 0)
        def _():
            wait_one(e_buf.at[b], e_ssem.at[b])

        return carry

    lax.fori_loop(0, blocks, finish, 0)

    def drain(j, carry):
        wait_all(csend_buf.at[j], c_ssem.at[j])

        def one(k, inner):
            wait_one(g_buf.at[first_own + j], g_ssem.at[j, k])
            return inner

        lax.fori_loop(1, stages, one, 0)
        return carry

    lax.fori_loop(0, own, drain, 0)
    each(0, blocks, lambda b: store_out(b).wait())


def hand_over(src_ref, dst_ref):
    dst_ref[...] = src_ref[...]


def body(tables, activations, cotangent, w_first, w_second, b_first):
    ranks = lax.axis_size("space")
    stages = lax.axis_size("pipe")
    _, rows, width, channels = activations.shape
    blocks, lanes = w_first.shape[2], w_first.shape[3]
    height = rows * ranks
    cols = width // 2 // ranks
    own = blocks // stages
    chunk = 2 * cols * rows
    tokens = height * cols
    sizes = (ranks, stages, blocks, lanes, height, width)
    vmem = pl.BlockSpec(memory_space=pltpu.VMEM)
    hbm = pl.BlockSpec(memory_space=pl.ANY)
    wire = (blocks, ranks, chunk, lanes)
    dma = pltpu.SemaphoreType.DMA
    out = pl.pallas_call(
        functools.partial(kernel, sizes),
        out_shape=jax.ShapeDtypeStruct((rows * width, channels), BF16),
        in_specs=[hbm] * 4 + [vmem] + [hbm] * 4 + [vmem],
        out_specs=hbm,
        scratch_shapes=[
            pltpu.VMEM((rows * width, channels), BF16),
            pltpu.VMEM((rows * width, channels), BF16),
            pltpu.VMEM(w_first.shape[1:], BF16),
            pltpu.VMEM(w_second.shape[1:], BF16),
            *[pltpu.VMEM(t.shape, BF16) for t in tables[:4]],
            dma((blocks,)),
            dma((blocks,)),
            dma((6,)),
            dma((blocks,)),
            pltpu.VMEM(wire, BF16),
            pltpu.VMEM(wire, BF16),
            pltpu.VMEM(wire, BF16),
            pltpu.VMEM((own,) + wire[1:], BF16),
            pltpu.VMEM((own,) + wire[1:], BF16),
            pltpu.VMEM((blocks, 2 * tokens, lanes), BF16),
            pltpu.VMEM((blocks, 2 * tokens, lanes), BF16),
            dma((blocks,)),
            dma((blocks,)),
            dma((blocks,)),
            dma((blocks,)),
            dma((own,)),
            dma((own,)),
            dma((own, stages)),
            dma((blocks,)),
            dma((blocks,)),
            dma((blocks,)),
        ],
        compiler_params=pltpu.CompilerParams(
            collective_id=0, has_side_effects=True, vmem_limit_bytes=62 * 1024 * 1024
        ),
    )(
        activations.reshape(rows * width, channels),
        cotangent.reshape(rows * width, channels),
        w_first[0],
        w_second[0],
        b_first,
        *tables,
    )
    tile = pl.BlockSpec((rows * width // 8, channels), lambda i: (i, 0))
    out = pl.pallas_call(
        hand_over,
        grid=(8,),
        out_shape=jax.ShapeDtypeStruct(out.shape, out.dtype),
        in_specs=[tile],
        out_specs=tile,
    )(out)
    return out.reshape(activations.shape)


def solution(mesh):
    ranks = mesh.shape["space"]

    def run(activations, cotangent, w_first, w_second, b_first):
        height, width = activations.shape[1], activations.shape[2]
        tables = dft_tables(height, width, width // 2, ranks)
        inner = jax.shard_map(
            body,
            mesh=mesh,
            in_specs=(
                [P()] * 5,
                P("pipe", "space", None, None),
                P("space", None, None),
                P("pipe", None, None, None, None),
                P("pipe", None, None, None, None),
                P("pipe", None, None),
            ),
            out_specs=P("pipe", "space", None, None),
            check_vma=False,
        )
        return inner(tables, activations, cotangent, w_first, w_second, b_first)

    return run
```
